32 devices in a mesh: groups: 2 (over y), dp: 4 (over z), tensor: 4 (over x, core).
Axes of the slice: x: 2, y: 2, z: 4, core: 2. Of those that a mesh axis runs over, the one named last changes fastest.
Arguments:
- acts: bfloat16 [16, 192, 8192], P(('groups', 'dp'), None, 'tensor'), parts along dimension 0, may hold values from -6 to 6
- grads: bfloat16 [16, 192, 28672], P(('groups', 'dp'), None, 'tensor'), parts along dimension 0, may hold values from -6 to 6
- in_basis: bfloat16 [64, 8192], P(None, 'tensor'), may hold values from -0.0625 to 0.0625
- out_basis: bfloat16 [64, 28672], P(None, 'tensor'), may hold values from -0.03125 to 0.03125
- queries: bfloat16 [256, 4096], P('dp'), may hold values from -0.09375 to 0.09375
- lengths: int32 [16], P(('groups', 'dp')), parts along dimension 0, may hold values from 1 to 192, as said below
Outputs:
- scores: float32 [16, 256], P(('groups', 'dp')), parts along dimension 0
The draws below stay inside these ranges and needn't reach their ends.
There are 2 independent parts, one for each index of `groups`. The reference program is written for one: setup_inputs(seed, part) draws one part's arguments, and reference() takes and returns one part's arrays. A program takes and returns all parts, laid end to end along the dimension named above; an argument that names none is the same for every part. Nothing has to cross between parts.
Inputs may be any that keep to these rules, and one draw needn't show every extreme that they name: `lengths`: the first example of every index of dp has all 192 tokens valid.
All inputs are finite; a program needn't handle non-finite values.
Results may differ from the reference program's by a relative error of at most 0.0029.
Values may be sent and summed in bfloat16 or wider, within the bound.
A program may use at most 64 MiB of HBM per device.

```python
import jax
import jax.numpy as jnp
from jax import lax

D = 8192
FF = 28672
RANK = 64
LEN = 192
E_DEV = 2
EXAMPLES = 8
QUERIES = 256


def draw_lengths(key, part):
    key = jax.random.fold_in(key, 7)
    drawn = jax.random.randint(key, (EXAMPLES,), 1, LEN + 1)
    firsts = jnp.arange(EXAMPLES) % E_DEV == 0
    return jnp.where(firsts, LEN, drawn).astype(jnp.int32)


def steps_of(own_key, shape, pieces, low, largest):
    loudness = 1.0
    for position, shards_of in pieces:
        draws = jax.random.uniform(jax.random.fold_in(jax.random.fold_in(own_key, 6), position), (shards_of,), jnp.float32, low / len(pieces), largest / len(pieces))
        loudness = loudness * jnp.repeat(jnp.exp(draws), shape[position] // shards_of).reshape((-1,) + (1,) * (len(shape) - 1 - position))
    return loudness


def normal_values(rng, dims, spread, most, pieces=(), dtype=jnp.bfloat16):
    array = spread * jax.random.normal(rng, dims, jnp.float32)
    if pieces:
        array = array * steps_of(rng, dims, pieces, -0.22, 0.18)
    return jnp.clip(array, -most, most).astype(dtype)


def setup_inputs(seed: int = 0, part: int = 0) -> dict:
    arg_keys = jax.random.split(jax.random.key(seed), 7)
    part_keys = jax.random.split(jax.random.fold_in(arg_keys[6], part), 7)
    acts = normal_values(part_keys[0], (EXAMPLES, LEN, D), 1.0, 6.0, ((0, 4), (2, 4)))
    grads = normal_values(part_keys[1], (EXAMPLES, LEN, FF), 1.0, 6.0, ((0, 4), (2, 4)))
    in_basis = normal_values(arg_keys[2], (RANK, D), D ** -0.5, 0.0625, ((1, 4),))
    out_basis = normal_values(arg_keys[3], (RANK, FF), FF ** -0.5, 0.03125, ((1, 4),))
    queries = normal_values(arg_keys[4], (QUERIES, RANK * RANK), (RANK * RANK) ** -0.5, 0.09375, ((0, 4),))
    lengths = draw_lengths(jax.random.fold_in(jax.random.fold_in(arg_keys[6], part), 71), part)
    return dict(acts=acts, grads=grads, in_basis=in_basis, out_basis=out_basis, queries=queries, lengths=lengths)


def reference(acts, grads, in_basis, out_basis, queries, lengths):

    def one_example(item):
        tokens, outgrad, count = item
        left = lax.dot_general(tokens, in_basis, (((1,), (1,)), ((), ())), preferred_element_type=jnp.float32)
        right = lax.dot_general(outgrad, out_basis, (((1,), (1,)), ((), ())), preferred_element_type=jnp.float32)
        keep = (jnp.arange(LEN) < count).astype(jnp.float32) * lax.rsqrt(count.astype(jnp.float32))
        return jnp.dot((right * keep[:, None]).T, left, precision=lax.Precision.HIGHEST, preferred_element_type=jnp.float32)
    sketches = lax.map(one_example, (acts, grads, lengths))
    flat = sketches.reshape(EXAMPLES, RANK * RANK).astype(jnp.bfloat16)
    return lax.dot_general(flat, queries, (((1,), (1,)), ((), ())), preferred_element_type=jnp.float32)
```

```python
import functools

import jax
import jax.numpy as jnp
from jax import lax
from jax.experimental import pallas as pl
from jax.experimental.pallas import tpu as pltpu
from jax.sharding import PartitionSpec as P

MESH = pl.DeviceIdType.MESH
NT = (((1,), (1,)), ((), ()))
LANES = 128


def each(start, stop, body):
    if stop - start <= 16:
        for s in range(start, stop):
            body(s)
    else:
        lax.fori_loop(start, stop, lambda s, c: (body(s), c)[1], 0)


def kernel(
    nd, n,
    acts, grads, in_basis, out_basis, queries, lengths,
    out,
    acts_v, grads_v, ib_v, ob_v, q_v,
    row_send, row_recv, sketch_v, part_v, part_recv, sum_v, score_send, score_recv,
    acts_sem, grads_sem, basis_sem, row_ssem, row_rsem, part_ssem, part_rsem, score_ssem, score_rsem,
):
    z = lax.axis_index("dp")
    k = lax.axis_index("tensor")
    e_dev, length, _ = acts.shape
    rank = in_basis.shape[0]
    parts = n // e_dev
    rows = length // parts
    mine, c = k // parts, lax.rem(k, parts)
    feats = q_v.shape[1]
    nq = queries.shape[0]
    peers = nd * n
    me = z * n + k

    def owner(s):
        return lax.rem(k + s, n)

    def fetch(src, dst, sem, s):
        b = owner(s)
        return pltpu.make_async_copy(
            src.at[b // parts, pl.ds(pl.multiple_of(lax.rem(b, parts) * rows, rows), rows), :],
            dst.at[s], sem.at[s])

    order = [s % n for s in range(1, n + 1)]
    get_ib = pltpu.make_async_copy(in_basis, ib_v, basis_sem.at[0])
    get_ob = pltpu.make_async_copy(out_basis, ob_v, basis_sem.at[1])
    get_q = pltpu.make_async_copy(
        queries.at[:, pl.ds(pl.multiple_of(c * feats, feats), feats)], q_v, basis_sem.at[2])
    get_ib.start()
    for s in order:
        fetch(acts, acts_v, acts_sem, s).start()
    get_ob.start()
    for s in order:
        fetch(grads, grads_v, grads_sem, s).start()
    get_q.start()

    barrier = pltpu.get_barrier_semaphore()

    def greet(s):
        to = lax.rem(me + s, peers)
        pl.semaphore_signal(
            barrier, inc=1, device_id={"dp": to // n, "tensor": lax.rem(to, n)}, device_id_type=MESH)

    each(1, peers, greet)

    def row_copy(s, side):
        return pltpu.make_async_remote_copy(
            src_ref=row_send.at[side, s], dst_ref=row_recv.at[side, s],
            send_sem=row_ssem.at[side, s], recv_sem=row_rsem.at[side, s],
            device_id={"tensor": owner(s)}, device_id_type=MESH)

    get_ib.wait()
    for s in order:
        fetch(acts, acts_v, acts_sem, s).wait()
        row_send[0, s] = lax.dot_general(ib_v[...], acts_v[s], NT, preferred_element_type=jnp.float32)
    pl.semaphore_wait(barrier, peers - 1)
    for s in range(1, n):
        row_copy(s, 0).start()

    get_ob.wait()
    for s in order:
        fetch(grads, grads_v, grads_sem, s).wait()
        row_send[1, s] = lax.dot_general(ob_v[...], grads_v[s], NT, preferred_element_type=jnp.float32)
        if s:
            row_copy(s, 1).start()

    left, right = row_send[0, 0], row_send[1, 0]
    for s in range(1, n):
        row_copy(s, 0).wait()
        left = left + row_recv[0, s]
    count = jnp.full((1, rows), lengths[mine], jnp.int32)
    place = c * rows + lax.broadcasted_iota(jnp.int32, (1, rows), 1)
    weight = jnp.where(place < count, lax.rsqrt(count.astype(jnp.float32)), 0.0)
    left = left * weight
    left = jnp.concatenate([left, left], axis=0)
    for s in range(1, n):
        row_copy(s, 1).wait()
        right = right + row_recv[1, s]
    sketch_v[...] = lax.dot_general(
        right, left, NT, precision=lax.Precision.HIGHEST, preferred_element_type=jnp.float32)

    lines = rank * rank // LANES
    per = LANES // rank
    lane = lax.broadcasted_iota(jnp.int32, (lines, LANES), 1)
    flat = sketch_v[pl.ds(0, lines, stride=per), :]
    for p in range(1, per):
        flat = jnp.where(lane < p * rank, flat, sketch_v[pl.ds(p, lines, stride=per), :])
    piece = lines // parts
    for p in range(parts):
        part_v[p] = flat[p * piece:(p + 1) * piece]

    group = nd * parts
    g = z * parts + c

    def part_copy(s, slot):
        to = lax.rem(g + s, group)
        return pltpu.make_async_remote_copy(
            src_ref=part_v.at[lax.rem(to, parts)], dst_ref=part_recv.at[slot],
            send_sem=part_ssem.at[s], recv_sem=part_rsem.at[s],
            device_id={"dp": to // parts, "tensor": mine * parts + lax.rem(to, parts)}, device_id_type=MESH)

    each(1, group, lambda s: part_copy(s, g).start())
    part_recv[g] = part_v[c]
    each(1, group, lambda s: part_copy(s, lax.rem(g - s + group, group)).wait())

    def add_parts(d):
        total = part_recv[d * parts]
        for p in range(1, parts):
            total = total + part_recv[d * parts + p]
        sum_v[pl.ds(d * piece, piece), :] = total

    for d in range(nd):
        add_parts(d)
    sketch = jnp.concatenate(
        [sum_v[pl.ds(r, nd, stride=piece), :] for r in range(piece)], axis=1).astype(jnp.bfloat16)
    get_q.wait()
    scores = lax.dot_general(sketch, q_v[...], NT, preferred_element_type=jnp.float32)

    width = score_send.shape[-1]
    fit = width // nq
    if fit > 1:
        scores = jnp.concatenate([scores] * fit, axis=1)
        lane = lax.broadcasted_iota(jnp.int32, scores.shape, 1)
        first = lax.rem(z, fit) * nq
        scores = jnp.where((lane >= first) & (lane < first + nq), scores, 0.0)
    for d in range(nd):
        score_send[d] = scores[d:d + 1]

    def score_copy(s, slot):
        to = lax.rem(me + s, peers)
        return pltpu.make_async_remote_copy(
            src_ref=score_send.at[to // n], dst_ref=score_recv.at[slot],
            send_sem=score_ssem.at[s], recv_sem=score_rsem.at[s],
            device_id={"dp": to // n, "tensor": lax.rem(to, n)}, device_id_type=MESH)

    each(1, peers, lambda s: score_copy(s, me).start())
    score_recv[me] = score_send[z]
    each(1, peers, lambda s: score_copy(s, lax.rem(me - s + peers, peers)).wait())
    for line in range(nd // fit):
        for e in range(e_dev):
            total = None
            for d in range(line * fit, (line + 1) * fit):
                for p in range(parts):
                    term = score_recv[d * n + e * parts + p]
                    total = term if total is None else total + term
            out[e:e + 1, line * width:(line + 1) * width] = total


def local(nd, n, acts, grads, in_basis, out_basis, queries, lengths):
    e_dev, length, ka = acts.shape
    kg = grads.shape[2]
    rank = in_basis.shape[0]
    parts = n // e_dev
    rows = length // parts
    nq, feats = queries.shape
    lines = rank * rank // LANES
    width = max(LANES, nq)
    f32, bf16 = jnp.float32, jnp.bfloat16
    hbm = pl.BlockSpec(memory_space=pl.ANY)
    dma = pltpu.SemaphoreType.DMA
    return pl.pallas_call(
        functools.partial(kernel, nd, n),
        out_shape=jax.ShapeDtypeStruct((e_dev, nd * nq), f32),
        in_specs=[hbm] * 5 + [pl.BlockSpec(memory_space=pltpu.SMEM)],
        out_specs=pl.BlockSpec(memory_space=pltpu.VMEM),
        scratch_shapes=[
            pltpu.VMEM((n, rows, ka), bf16),
            pltpu.VMEM((n, rows, kg), bf16),
            pltpu.VMEM((rank, ka), bf16),
            pltpu.VMEM((rank, kg), bf16),
            pltpu.VMEM((nq, feats // parts), bf16),
            pltpu.VMEM((2, n, rank, rows), f32),
            pltpu.VMEM((2, n, rank, rows), f32),
            pltpu.VMEM((rank, LANES), f32),
            pltpu.VMEM((parts, lines // parts, LANES), f32),
            pltpu.VMEM((nd * parts, lines // parts, LANES), f32),
            pltpu.VMEM((nd * lines // parts, LANES), f32),
            pltpu.VMEM((nd, 1, width), f32),
            pltpu.VMEM((nd * n, 1, width), f32),
            dma((n,)),
            dma((n,)),
            dma((3,)),
            dma((2, n)),
            dma((2, n)),
            dma((nd * parts,)),
            dma((nd * parts,)),
            dma((nd * n,)),
            dma((nd * n,)),
        ],
        compiler_params=pltpu.CompilerParams(
            collective_id=0, has_side_effects=True, vmem_limit_bytes=48 * 2**20),
        cost_estimate=pl.CostEstimate(
            flops=2 * e_dev * length * rank * (ka + kg),
            bytes_accessed=2 * (e_dev * length + rank) * (ka + kg) + 2 * nq * feats // parts,
            transcendentals=0),
    )(acts, grads, in_basis, out_basis, queries, lengths)


def solution(mesh):
    nd, n = mesh.shape["dp"], mesh.shape["tensor"]
    in_specs = (
        P(("groups", "dp"), None, "tensor"),
        P(("groups", "dp"), None, "tensor"),
        P(None, "tensor"),
        P(None, "tensor"),
        P("dp", None),
        P(("groups", "dp")),
    )
    out_specs = P(("groups", "dp"), None)
    return jax.shard_map(
        functools.partial(local, nd, n), mesh=mesh, in_specs=in_specs, out_specs=out_specs, check_vma=False)
```

```python
import functools

import jax
import jax.numpy as jnp
from jax import lax
from jax.experimental import pallas as pl
from jax.experimental.pallas import tpu as pltpu
from jax.sharding import PartitionSpec as P

MESH = pl.DeviceIdType.MESH
NT = (((1,), (1,)), ((), ()))
LANES = 128
DEPTH = 2
HELD = 1


def each(start, stop, body):
    if stop - start <= 16:
        for s in range(start, stop):
            body(s)
    else:
        lax.fori_loop(start, stop, lambda s, c: (body(s), c)[1], 0)


def kernel(
    nd, n,
    acts, grads, in_basis, out_basis, queries, lengths,
    out,
    acts_v, grads_v, ib_v, ob_v, q_v, len_v,
    row_send, row_recv, sketch_v, part_v, part_recv, sum_v, score_send, score_recv,
    acts_sem, grads_sem, basis_sem, row_ssem, row_rsem, part_ssem, part_rsem, score_ssem, score_rsem,
):
    z = lax.axis_index("dp")
    k = lax.axis_index("tensor")
    e_dev, length, _ = acts.shape
    rank = in_basis.shape[0]
    parts = n // e_dev
    rows = length // parts
    mine, c = k // parts, lax.rem(k, parts)
    feats = q_v.shape[1]
    nq = queries.shape[0]
    peers = nd * n
    me = z * n + k

    def owner(s):
        return lax.rem(k + s, n)

    def fetch(src, dst, sem, s):
        b = owner(s)
        return pltpu.make_async_copy(
            src.at[b // parts, pl.ds(pl.multiple_of(lax.rem(b, parts) * rows, rows), rows), :],
            dst.at[s], sem.at[s])

    order = [s % n for s in range(1, n + 1)]
    get_ib = pltpu.make_async_copy(in_basis, ib_v, basis_sem.at[0])
    get_ob = pltpu.make_async_copy(out_basis, ob_v, basis_sem.at[1])
    get_q = pltpu.make_async_copy(
        queries.at[:, pl.ds(pl.multiple_of(c * feats, feats), feats)], q_v, basis_sem.at[2])
    get_len = pltpu.make_async_copy(lengths, len_v, basis_sem.at[3])
    get_ib.start()
    for s in order:
        fetch(acts, acts_v, acts_sem, s).start()
    get_ob.start()
    for s in order[:DEPTH]:
        fetch(grads, grads_v, grads_sem, s).start()

    barrier = pltpu.get_barrier_semaphore()

    def greet(s):
        to = lax.rem(me + s, peers)
        pl.semaphore_signal(
            barrier, inc=1, device_id={"dp": to // n, "tensor": lax.rem(to, n)}, device_id_type=MESH)

    each(1, peers, greet)

    def row_copy(s, side):
        return pltpu.make_async_remote_copy(
            src_ref=row_send.at[side, s], dst_ref=row_recv.at[side, s],
            send_sem=row_ssem.at[side, s], recv_sem=row_rsem.at[side, s],
            device_id={"tensor": owner(s)}, device_id_type=MESH)

    get_ib.wait()
    for s in order:
        fetch(acts, acts_v, acts_sem, s).wait()
        row_send[0, s] = lax.dot_general(ib_v[...], acts_v[s], NT, preferred_element_type=jnp.float32)
    get_ob.wait()
    for i, s in enumerate(order):
        fetch(grads, grads_v, grads_sem, s).wait()
        if i + DEPTH < n:
            fetch(grads, grads_v, grads_sem, order[i + DEPTH]).start()
        elif i == n - 1:
            get_q.start()
            get_len.start()
        row_send[1, s] = lax.dot_general(ob_v[...], grads_v[s], NT, preferred_element_type=jnp.float32)
        if i == HELD:
            pl.semaphore_wait(barrier, peers - 1)
            for t in range(1, n):
                row_copy(t, 0).start()
            for t in order[:i + 1]:
                if t:
                    row_copy(t, 1).start()
        elif i > HELD and s:
            row_copy(s, 1).start()

    left, right = row_send[0, 0], row_send[1, 0]
    for s in range(1, n):
        row_copy(s, 0).wait_recv()
        left = left + row_recv[0, s]
    get_len.wait()
    count = jnp.full((1, rows), len_v[mine], jnp.int32)
    place = c * rows + lax.broadcasted_iota(jnp.int32, (1, rows), 1)
    weight = jnp.where(place < count, lax.rsqrt(count.astype(jnp.float32)), 0.0)
    left = left * weight
    left = jnp.concatenate([left, left], axis=0)
    for s in range(1, n):
        row_copy(s, 1).wait_recv()
        right = right + row_recv[1, s]
    sketch_v[...] = lax.dot_general(
        right, left, NT, precision=lax.Precision.HIGHEST, preferred_element_type=jnp.float32)

    lines = rank * rank // LANES
    per = LANES // rank
    lane = lax.broadcasted_iota(jnp.int32, (lines, LANES), 1)
    flat = sketch_v[pl.ds(0, lines, stride=per), :]
    for p in range(1, per):
        flat = jnp.where(lane < p * rank, flat, sketch_v[pl.ds(p, lines, stride=per), :])
    piece = lines // parts
    for p in range(parts):
        part_v[p] = flat[p * piece:(p + 1) * piece]

    group = nd * parts
    g = z * parts + c

    def part_copy(s, slot):
        to = lax.rem(g + s, group)
        return pltpu.make_async_remote_copy(
            src_ref=part_v.at[lax.rem(to, parts)], dst_ref=part_recv.at[slot],
            send_sem=part_ssem.at[s], recv_sem=part_rsem.at[s],
            device_id={"dp": to // parts, "tensor": mine * parts + lax.rem(to, parts)}, device_id_type=MESH)

    each(1, group, lambda s: part_copy(s, g).start())
    part_recv[g] = part_v[c]
    each(1, group, lambda s: part_copy(s, lax.rem(g - s + group, group)).wait_recv())

    def add_parts(d):
        total = part_recv[d * parts]
        for p in range(1, parts):
            total = total + part_recv[d * parts + p]
        sum_v[pl.ds(d * piece, piece), :] = total

    for d in range(nd):
        add_parts(d)
    sketch = jnp.concatenate(
        [sum_v[pl.ds(r, nd, stride=piece), :] for r in range(piece)], axis=1).astype(jnp.bfloat16)
    get_q.wait()
    scores = lax.dot_general(sketch, q_v[...], NT, preferred_element_type=jnp.float32)

    width = score_send.shape[-1]
    fit = width // nq
    if fit > 1:
        scores = jnp.concatenate([scores] * fit, axis=1)
        lane = lax.broadcasted_iota(jnp.int32, scores.shape, 1)
        first = lax.rem(z, fit) * nq
        scores = jnp.where((lane >= first) & (lane < first + nq), scores, 0.0)
    for d in range(nd):
        score_send[d] = scores[d:d + 1]

    def score_copy(s, slot):
        to = lax.rem(me + s, peers)
        return pltpu.make_async_remote_copy(
            src_ref=score_send.at[to // n], dst_ref=score_recv.at[slot],
            send_sem=score_ssem.at[s], recv_sem=score_rsem.at[s],
            device_id={"dp": to // n, "tensor": lax.rem(to, n)}, device_id_type=MESH)

    each(1, peers, lambda s: score_copy(s, me).start())
    score_recv[me] = score_send[z]
    each(1, peers, lambda s: score_copy(s, lax.rem(me - s + peers, peers)).wait_recv())
    for line in range(nd // fit):
        for e in range(e_dev):
            total = None
            for d in range(line * fit, (line + 1) * fit):
                for p in range(parts):
                    term = score_recv[d * n + e * parts + p]
                    total = term if total is None else total + term
            out[e:e + 1, line * width:(line + 1) * width] = total

    for s in range(1, n):
        row_copy(s, 0).wait_send()
        row_copy(s, 1).wait_send()
    each(1, group, lambda s: part_copy(s, g).wait_send())
    each(1, peers, lambda s: score_copy(s, me).wait_send())


def local(nd, n, acts, grads, in_basis, out_basis, queries, lengths):
    e_dev, length, ka = acts.shape
    kg = grads.shape[2]
    rank = in_basis.shape[0]
    parts = n // e_dev
    rows = length // parts
    nq, feats = queries.shape
    lines = rank * rank // LANES
    width = max(LANES, nq)
    f32, bf16 = jnp.float32, jnp.bfloat16
    hbm = pl.BlockSpec(memory_space=pltpu.HBM)
    dma = pltpu.SemaphoreType.DMA
    return pl.pallas_call(
        functools.partial(kernel, nd, n),
        out_shape=jax.ShapeDtypeStruct((e_dev, nd * nq), f32),
        in_specs=[hbm] * 6,
        out_specs=pl.BlockSpec(memory_space=pltpu.VMEM),
        scratch_shapes=[
            pltpu.VMEM((n, rows, ka), bf16),
            pltpu.VMEM((n, rows, kg), bf16),
            pltpu.VMEM((rank, ka), bf16),
            pltpu.VMEM((rank, kg), bf16),
            pltpu.VMEM((nq, feats // parts), bf16),
            pltpu.SMEM((e_dev,), jnp.int32),
            pltpu.VMEM((2, n, rank, rows), f32),
            pltpu.VMEM((2, n, rank, rows), f32),
            pltpu.VMEM((rank, LANES), f32),
            pltpu.VMEM((parts, lines // parts, LANES), f32),
            pltpu.VMEM((nd * parts, lines // parts, LANES), f32),
            pltpu.VMEM((nd * lines // parts, LANES), f32),
            pltpu.VMEM((nd, 1, width), f32),
            pltpu.VMEM((nd * n, 1, width), f32),
            dma((n,)),
            dma((n,)),
            dma((4,)),
            dma((2, n)),
            dma((2, n)),
            dma((nd * parts,)),
            dma((nd * parts,)),
            dma((nd * n,)),
            dma((nd * n,)),
        ],
        compiler_params=pltpu.CompilerParams(
            collective_id=0, has_side_effects=True, vmem_limit_bytes=60 * 2**20),
        cost_estimate=pl.CostEstimate(
            flops=2 * e_dev * length * rank * (ka + kg),
            bytes_accessed=2 * (e_dev * length + rank) * (ka + kg) + 2 * nq * feats // parts,
            transcendentals=0),
    )(acts, grads, in_basis, out_basis, queries, lengths)


def solution(mesh):
    nd, n = mesh.shape["dp"], mesh.shape["tensor"]
    in_specs = (
        P(("groups", "dp"), None, "tensor"),
        P(("groups", "dp"), None, "tensor"),
        P(None, "tensor"),
        P(None, "tensor"),
        P("dp", None),
        P(("groups", "dp")),
    )
    out_specs = P(("groups", "dp"), None)
    return jax.shard_map(
        functools.partial(local, nd, n), mesh=mesh, in_specs=in_specs, out_specs=out_specs, check_vma=False)
```

```python
import functools

import jax
import jax.numpy as jnp
from jax import lax
from jax.experimental import pallas as pl
from jax.experimental.pallas import tpu as pltpu
from jax.sharding import PartitionSpec as P

MESH = pl.DeviceIdType.MESH
NT = (((1,), (1,)), ((), ()))
LANES = 128
DEPTH = 2
HELD = 1


def each(start, stop, body):
    if stop - start <= 16:
        for s in range(start, stop):
            body(s)
    else:
        lax.fori_loop(start, stop, lambda s, c: (body(s), c)[1], 0)


def kernel(
    nd, n,
    acts, grads, in_basis, out_basis, queries, lengths,
    out,
    acts_v, grads_v, ib_v, ob_v, q_v, len_v,
    row_send, row_recv, sketch_v, part_v, part_recv, sum_v, score_send, score_recv,
    acts_sem, grads_sem, basis_sem, row_ssem, row_rsem, part_ssem, part_rsem, score_ssem, score_rsem,
):
    z = lax.axis_index("dp")
    k = lax.axis_index("tensor")
    e_dev, length, _ = acts.shape
    rank = in_basis.shape[0]
    parts = n // e_dev
    rows = length // parts
    mine, c = k // parts, lax.rem(k, parts)
    feats = q_v.shape[1]
    nq = queries.shape[0]
    peers = nd * n
    me = z * n + k

    half = lax.rem(k, 2)

    def owner(s):
        pair, flip = s // 2, s % 2
        return lax.rem(k // 2 + pair, n // 2) * 2 + (lax.rem(half + 1, 2) if flip else half)

    def fetch(src, dst, sem, s):
        b = owner(s)
        return pltpu.make_async_copy(
            src.at[b // parts, pl.ds(pl.multiple_of(lax.rem(b, parts) * rows, rows), rows), :],
            dst.at[s], sem.at[s])

    order = [s for s in range(2, n)] + [1, 0]
    get_ib = pltpu.make_async_copy(in_basis, ib_v, basis_sem.at[0])
    get_ob = pltpu.make_async_copy(out_basis, ob_v, basis_sem.at[1])
    get_q = pltpu.make_async_copy(
        queries.at[:, pl.ds(pl.multiple_of(c * feats, feats), feats)], q_v, basis_sem.at[2])
    get_len = pltpu.make_async_copy(lengths, len_v, basis_sem.at[3])
    get_ib.start()
    for s in order:
        fetch(acts, acts_v, acts_sem, s).start()
    get_ob.start()
    for s in order[:DEPTH]:
        fetch(grads, grads_v, grads_sem, s).start()

    barrier = pltpu.get_barrier_semaphore()

    def greet(s):
        to = lax.rem(me + s, peers)
        pl.semaphore_signal(
            barrier, inc=1, device_id={"dp": to // n, "tensor": lax.rem(to, n)}, device_id_type=MESH)

    each(1, peers, greet)

    def row_copy(s):
        return pltpu.make_async_remote_copy(
            src_ref=row_send.at[s], dst_ref=row_recv.at[s],
            send_sem=row_ssem.at[s], recv_sem=row_rsem.at[s],
            device_id={"tensor": owner(s)}, device_id_type=MESH)

    get_ib.wait()
    for s in order:
        fetch(acts, acts_v, acts_sem, s).wait()
        row_send[s, :, :rank] = lax.dot_general(acts_v[s], ib_v[...], NT, preferred_element_type=jnp.float32)
    get_ob.wait()
    for i, s in enumerate(order):
        fetch(grads, grads_v, grads_sem, s).wait()
        if i + DEPTH < n:
            fetch(grads, grads_v, grads_sem, order[i + DEPTH]).start()
        elif i == n - 1:
            get_q.start()
            get_len.start()
        row_send[s, :, rank:] = lax.dot_general(grads_v[s], ob_v[...], NT, preferred_element_type=jnp.float32)
        if i == HELD:
            pl.semaphore_wait(barrier, peers - 1)
            for t in order[:i + 1]:
                if t:
                    row_copy(t).start()
        elif i > HELD and s:
            row_copy(s).start()

    both = row_send[0]
    for s in order[:-1]:
        row_copy(s).wait_recv()
        both = both + row_recv[s]
    get_len.wait()
    count = jnp.full((rows, 2 * rank), len_v[mine], jnp.int32)
    place = c * rows + lax.broadcasted_iota(jnp.int32, (rows, 2 * rank), 0)
    weight = jnp.where(place < count, lax.rsqrt(count.astype(jnp.float32)), 0.0)
    left, right = both[:, :rank] * weight[:, :rank], both[:, rank:]
    left = jnp.concatenate([left, left], axis=1)
    sketch_v[...] = lax.dot_general(
        right, left, (((0,), (0,)), ((), ())), precision=lax.Precision.HIGHEST, preferred_element_type=jnp.float32)

    lines = rank * rank // LANES
    per = LANES // rank
    lane = lax.broadcasted_iota(jnp.int32, (lines, LANES), 1)
    flat = sketch_v[pl.ds(0, lines, stride=per), :]
    for p in range(1, per):
        flat = jnp.where(lane < p * rank, flat, sketch_v[pl.ds(p, lines, stride=per), :])
    piece = lines // parts
    for p in range(parts):
        part_v[p] = flat[p * piece:(p + 1) * piece]

    group = nd * parts
    g = z * parts + c

    def part_copy(s, slot):
        to = lax.rem(g + s, group)
        return pltpu.make_async_remote_copy(
            src_ref=part_v.at[lax.rem(to, parts)], dst_ref=part_recv.at[slot],
            send_sem=part_ssem.at[s], recv_sem=part_rsem.at[s],
            device_id={"dp": to // parts, "tensor": mine * parts + lax.rem(to, parts)}, device_id_type=MESH)

    each(1, group, lambda s: part_copy(s, g).start())
    part_recv[g] = part_v[c]
    each(1, group, lambda s: part_copy(s, lax.rem(g - s + group, group)).wait_recv())

    def add_parts(d):
        total = part_recv[d * parts]
        for p in range(1, parts):
            total = total + part_recv[d * parts + p]
        sum_v[pl.ds(d * piece, piece), :] = total

    for d in range(nd):
        add_parts(d)
    sketch = jnp.concatenate(
        [sum_v[pl.ds(r, nd, stride=piece), :] for r in range(piece)], axis=1).astype(jnp.bfloat16)
    get_q.wait()
    scores = lax.dot_general(sketch, q_v[...], NT, preferred_element_type=jnp.float32)

    width = score_send.shape[-1]
    fit = width // nq
    if fit > 1:
        scores = jnp.concatenate([scores] * fit, axis=1)
        lane = lax.broadcasted_iota(jnp.int32, scores.shape, 1)
        first = lax.rem(z, fit) * nq
        scores = jnp.where((lane >= first) & (lane < first + nq), scores, 0.0)
    for d in range(nd):
        score_send[d] = scores[d:d + 1]

    def score_copy(s, slot):
        to = lax.rem(me + s, peers)
        return pltpu.make_async_remote_copy(
            src_ref=score_send.at[to // n], dst_ref=score_recv.at[slot],
            send_sem=score_ssem.at[s], recv_sem=score_rsem.at[s],
            device_id={"dp": to // n, "tensor": lax.rem(to, n)}, device_id_type=MESH)

    each(1, peers, lambda s: score_copy(s, me).start())
    score_recv[me] = score_send[z]
    each(1, peers, lambda s: score_copy(s, lax.rem(me - s + peers, peers)).wait_recv())
    for line in range(nd // fit):
        for e in range(e_dev):
            total = None
            for d in range(line * fit, (line + 1) * fit):
                for p in range(parts):
                    term = score_recv[d * n + e * parts + p]
                    total = term if total is None else total + term
            out[e:e + 1, line * width:(line + 1) * width] = total

    for s in range(1, n):
        row_copy(s).wait_send()
    each(1, group, lambda s: part_copy(s, g).wait_send())
    each(1, peers, lambda s: score_copy(s, me).wait_send())


def local(nd, n, acts, grads, in_basis, out_basis, queries, lengths):
    e_dev, length, ka = acts.shape
    kg = grads.shape[2]
    rank = in_basis.shape[0]
    parts = n // e_dev
    rows = length // parts
    nq, feats = queries.shape
    lines = rank * rank // LANES
    width = max(LANES, nq)
    f32, bf16 = jnp.float32, jnp.bfloat16
    hbm = pl.BlockSpec(memory_space=pltpu.HBM)
    dma = pltpu.SemaphoreType.DMA
    return pl.pallas_call(
        functools.partial(kernel, nd, n),
        out_shape=jax.ShapeDtypeStruct((e_dev, nd * nq), f32),
        in_specs=[hbm] * 6,
        out_specs=pl.BlockSpec(memory_space=pltpu.VMEM),
        scratch_shapes=[
            pltpu.VMEM((n, rows, ka), bf16),
            pltpu.VMEM((n, rows, kg), bf16),
            pltpu.VMEM((rank, ka), bf16),
            pltpu.VMEM((rank, kg), bf16),
            pltpu.VMEM((nq, feats // parts), bf16),
            pltpu.SMEM((e_dev,), jnp.int32),
            pltpu.VMEM((n, rows, 2 * rank), f32),
            pltpu.VMEM((n, rows, 2 * rank), f32),
            pltpu.VMEM((rank, LANES), f32),
            pltpu.VMEM((parts, lines // parts, LANES), f32),
            pltpu.VMEM((nd * parts, lines // parts, LANES), f32),
            pltpu.VMEM((nd * lines // parts, LANES), f32),
            pltpu.VMEM((nd, 1, width), f32),
            pltpu.VMEM((nd * n, 1, width), f32),
            dma((n,)),
            dma((n,)),
            dma((4,)),
            dma((n,)),
            dma((n,)),
            dma((nd * parts,)),
            dma((nd * parts,)),
            dma((nd * n,)),
            dma((nd * n,)),
        ],
        compiler_params=pltpu.CompilerParams(
            collective_id=0, has_side_effects=True, vmem_limit_bytes=60 * 2**20),
        cost_estimate=pl.CostEstimate(
            flops=2 * e_dev * length * rank * (ka + kg),
            bytes_accessed=2 * (e_dev * length + rank) * (ka + kg) + 2 * nq * feats // parts,
            transcendentals=0),
    )(acts, grads, in_basis, out_basis, queries, lengths)


def solution(mesh):
    nd, n = mesh.shape["dp"], mesh.shape["tensor"]
    in_specs = (
        P(("groups", "dp"), None, "tensor"),
        P(("groups", "dp"), None, "tensor"),
        P(None, "tensor"),
        P(None, "tensor"),
        P("dp", None),
        P(("groups", "dp")),
    )
    out_specs = P(("groups", "dp"), None)
    return jax.shard_map(
        functools.partial(local, nd, n), mesh=mesh, in_specs=in_specs, out_specs=out_specs, check_vma=False)
```

```python
import functools

import jax
import jax.numpy as jnp
from jax import lax
from jax.experimental import pallas as pl
from jax.experimental.pallas import tpu as pltpu
from jax.sharding import PartitionSpec as P

MESH = pl.DeviceIdType.MESH
NT = (((1,), (1,)), ((), ()))
LANES = 128
DEPTH = 2
HELD = 0


def each(start, stop, body):
    if stop - start <= 16:
        for s in reversed(range(start, stop)):
            body(s)
    else:
        lax.fori_loop(start, stop, lambda s, c: (body(s), c)[1], 0)


def to_at(a, s, count):
    if not isinstance(s, int) or count & (count - 1):
        return lax.rem(a + s, count)
    bit, to = 1, a
    while bit < count:
        if s & bit:
            to = to + bit - 2 * bit * lax.rem(a // bit, 2)
        bit *= 2
    return to


def from_at(a, s, count):
    if not isinstance(s, int) or count & (count - 1):
        return lax.rem(a - s + count, count)
    return to_at(a, s, count)


def kernel(
    nd, n,
    acts, grads, in_basis, out_basis, queries, lengths,
    out,
    acts_v, grads_v, ib_v, ob_v, q_v, len_v,
    row_send, row_recv, sketch_v, part_v, part_recv, sum_v, score_send, score_recv,
    acts_sem, grads_sem, basis_sem, row_ssem, row_rsem, part_ssem, part_rsem, score_ssem, score_rsem,
):
    z = lax.axis_index("dp")
    k = lax.axis_index("tensor")
    e_dev, length, _ = acts.shape
    rank = in_basis.shape[0]
    parts = n // e_dev
    rows = length // parts
    mine, c = k // parts, lax.rem(k, parts)
    feats = q_v.shape[1]
    nq = queries.shape[0]
    peers = nd * n
    me = z * n + k

    half = lax.rem(k, 2)

    def owner(s):
        pair, flip = s // 2, s % 2
        return lax.rem(k // 2 + pair, n // 2) * 2 + (lax.rem(half + 1, 2) if flip else half)

    def fetch(src, dst, sem, s):
        b = owner(s)
        return pltpu.make_async_copy(
            src.at[b // parts, pl.ds(pl.multiple_of(lax.rem(b, parts) * rows, rows), rows), :],
            dst.at[s], sem.at[s])

    order = [s for s in range(2, n)] + [1, 0]
    get_ib = pltpu.make_async_copy(in_basis, ib_v, basis_sem.at[0])
    get_ob = pltpu.make_async_copy(out_basis, ob_v, basis_sem.at[1])
    get_q = pltpu.make_async_copy(
        queries.at[:, pl.ds(pl.multiple_of(c * feats, feats), feats)], q_v, basis_sem.at[2])
    get_len = pltpu.make_async_copy(lengths, len_v, basis_sem.at[3])
    get_ib.start()
    for s in order:
        fetch(acts, acts_v, acts_sem, s).start()
    get_ob.start()
    for s in order[:DEPTH]:
        fetch(grads, grads_v, grads_sem, s).start()

    barrier = pltpu.get_barrier_semaphore()

    def greet(s):
        to = to_at(me, s, peers)
        pl.semaphore_signal(
            barrier, inc=1, device_id={"dp": to // n, "tensor": lax.rem(to, n)}, device_id_type=MESH)

    each(1, peers, greet)

    def row_copy(s):
        return pltpu.make_async_remote_copy(
            src_ref=row_send.at[s], dst_ref=row_recv.at[s],
            send_sem=row_ssem.at[s], recv_sem=row_rsem.at[s],
            device_id={"tensor": owner(s)}, device_id_type=MESH)

    get_ib.wait()
    for s in order:
        fetch(acts, acts_v, acts_sem, s).wait()
        row_send[s, :, :rank] = lax.dot_general(acts_v[s], ib_v[...], NT, preferred_element_type=jnp.float32)
    get_ob.wait()
    for i, s in enumerate(order):
        fetch(grads, grads_v, grads_sem, s).wait()
        if i + DEPTH < n:
            fetch(grads, grads_v, grads_sem, order[i + DEPTH]).start()
        elif i == n - 1:
            get_q.start()
            get_len.start()
        row_send[s, :, rank:] = lax.dot_general(grads_v[s], ob_v[...], NT, preferred_element_type=jnp.float32)
        if i == HELD:
            pl.semaphore_wait(barrier, peers - 1)
            for t in order[:i + 1]:
                if t:
                    row_copy(t).start()
        elif i > HELD and s:
            row_copy(s).start()

    both = row_send[0]
    for s in order[:-1]:
        row_copy(s).wait_recv()
        both = both + row_recv[s]
    get_len.wait()
    count = jnp.full((rows, 2 * rank), len_v[mine], jnp.int32)
    place = c * rows + lax.broadcasted_iota(jnp.int32, (rows, 2 * rank), 0)
    weight = jnp.where(place < count, lax.rsqrt(count.astype(jnp.float32)), 0.0)
    left, right = both[:, :rank] * weight[:, :rank], both[:, rank:]
    left = jnp.concatenate([left, left], axis=1)
    sketch_v[...] = lax.dot_general(
        right, left, (((0,), (0,)), ((), ())), precision=lax.Precision.HIGHEST, preferred_element_type=jnp.float32)

    lines = rank * rank // LANES
    per = LANES // rank
    lane = lax.broadcasted_iota(jnp.int32, (lines, LANES), 1)
    flat = sketch_v[pl.ds(0, lines, stride=per), :]
    for p in range(1, per):
        flat = jnp.where(lane < p * rank, flat, sketch_v[pl.ds(p, lines, stride=per), :])
    piece = lines // parts
    for p in range(parts):
        part_v[p] = flat[p * piece:(p + 1) * piece]

    group = nd * parts
    g = z * parts + c

    def part_copy(s, slot):
        to = to_at(g, s, group)
        return pltpu.make_async_remote_copy(
            src_ref=part_v.at[lax.rem(to, parts)], dst_ref=part_recv.at[slot],
            send_sem=part_ssem.at[s], recv_sem=part_rsem.at[s],
            device_id={"dp": to // parts, "tensor": mine * parts + lax.rem(to, parts)}, device_id_type=MESH)

    each(1, group, lambda s: part_copy(s, g).start())
    part_recv[g] = part_v[c]
    each(1, group, lambda s: part_copy(s, from_at(g, s, group)).wait_recv())

    def add_parts(d):
        total = part_recv[d * parts]
        for p in range(1, parts):
            total = total + part_recv[d * parts + p]
        sum_v[pl.ds(d * piece, piece), :] = total

    for d in range(nd):
        add_parts(d)
    sketch = jnp.concatenate(
        [sum_v[pl.ds(r, nd, stride=piece), :] for r in range(piece)], axis=1).astype(jnp.bfloat16)
    get_q.wait()
    scores = lax.dot_general(sketch, q_v[...], NT, preferred_element_type=jnp.float32)

    width = score_send.shape[-1]
    fit = width // nq
    if fit > 1:
        scores = jnp.concatenate([scores] * fit, axis=1)
        lane = lax.broadcasted_iota(jnp.int32, scores.shape, 1)
        first = lax.rem(z, fit) * nq
        scores = jnp.where((lane >= first) & (lane < first + nq), scores, 0.0)
    for d in range(nd):
        score_send[d] = scores[d:d + 1]

    def score_copy(s, slot):
        to = to_at(me, s, peers)
        return pltpu.make_async_remote_copy(
            src_ref=score_send.at[to // n], dst_ref=score_recv.at[slot],
            send_sem=score_ssem.at[s], recv_sem=score_rsem.at[s],
            device_id={"dp": to // n, "tensor": lax.rem(to, n)}, device_id_type=MESH)

    each(1, peers, lambda s: score_copy(s, me).start())
    score_recv[me] = score_send[z]
    each(1, peers, lambda s: score_copy(s, from_at(me, s, peers)).wait_recv())
    for line in range(nd // fit):
        for e in range(e_dev):
            total = None
            for d in range(line * fit, (line + 1) * fit):
                for p in range(parts):
                    term = score_recv[d * n + e * parts + p]
                    total = term if total is None else total + term
            out[e:e + 1, line * width:(line + 1) * width] = total

    for s in range(1, n):
        row_copy(s).wait_send()
    each(1, group, lambda s: part_copy(s, g).wait_send())
    each(1, peers, lambda s: score_copy(s, me).wait_send())


def local(nd, n, acts, grads, in_basis, out_basis, queries, lengths):
    e_dev, length, ka = acts.shape
    kg = grads.shape[2]
    rank = in_basis.shape[0]
    parts = n // e_dev
    rows = length // parts
    nq, feats = queries.shape
    lines = rank * rank // LANES
    width = max(LANES, nq)
    f32, bf16 = jnp.float32, jnp.bfloat16
    hbm = pl.BlockSpec(memory_space=pltpu.HBM)
    dma = pltpu.SemaphoreType.DMA
    return pl.pallas_call(
        functools.partial(kernel, nd, n),
        out_shape=jax.ShapeDtypeStruct((e_dev, nd * nq), f32),
        in_specs=[hbm] * 6,
        out_specs=pl.BlockSpec(memory_space=pltpu.VMEM),
        scratch_shapes=[
            pltpu.VMEM((n, rows, ka), bf16),
            pltpu.VMEM((n, rows, kg), bf16),
            pltpu.VMEM((rank, ka), bf16),
            pltpu.VMEM((rank, kg), bf16),
            pltpu.VMEM((nq, feats // parts), bf16),
            pltpu.SMEM((e_dev,), jnp.int32),
            pltpu.VMEM((n, rows, 2 * rank), f32),
            pltpu.VMEM((n, rows, 2 * rank), f32),
            pltpu.VMEM((rank, LANES), f32),
            pltpu.VMEM((parts, lines // parts, LANES), f32),
            pltpu.VMEM((nd * parts, lines // parts, LANES), f32),
            pltpu.VMEM((nd * lines // parts, LANES), f32),
            pltpu.VMEM((nd, 1, width), f32),
            pltpu.VMEM((nd * n, 1, width), f32),
            dma((n,)),
            dma((n,)),
            dma((4,)),
            dma((n,)),
            dma((n,)),
            dma((nd * parts,)),
            dma((nd * parts,)),
            dma((nd * n,)),
            dma((nd * n,)),
        ],
        compiler_params=pltpu.CompilerParams(
            collective_id=0, has_side_effects=True, vmem_limit_bytes=60 * 2**20),
        cost_estimate=pl.CostEstimate(
            flops=2 * e_dev * length * rank * (ka + kg),
            bytes_accessed=2 * (e_dev * length + rank) * (ka + kg) + 2 * nq * feats // parts,
            transcendentals=0),
    )(acts, grads, in_basis, out_basis, queries, lengths)


def solution(mesh):
    nd, n = mesh.shape["dp"], mesh.shape["tensor"]
    in_specs = (
        P(("groups", "dp"), None, "tensor"),
        P(("groups", "dp"), None, "tensor"),
        P(None, "tensor"),
        P(None, "tensor"),
        P("dp", None),
        P(("groups", "dp")),
    )
    out_specs = P(("groups", "dp"), None)
    return jax.shard_map(
        functools.partial(local, nd, n), mesh=mesh, in_specs=in_specs, out_specs=out_specs, check_vma=False)
```

```python
import functools

import jax
import jax.numpy as jnp
from jax import lax
from jax.experimental import pallas as pl
from jax.experimental.pallas import tpu as pltpu
from jax.sharding import PartitionSpec as P

MESH = pl.DeviceIdType.MESH
NT = (((1,), (1,)), ((), ()))
LANES = 128
DEPTH = 2
HELD = 0


def each(start, stop, body):
    if stop - start <= 16:
        for s in reversed(range(start, stop)):
            body(s)
    else:
        lax.fori_loop(start, stop, lambda s, c: (body(s), c)[1], 0)


def to_at(a, s, count):
    if not isinstance(s, int) or count & (count - 1):
        return lax.rem(a + s, count)
    bit, to = 1, a
    while bit < count:
        if s & bit:
            to = to + bit - 2 * bit * lax.rem(a // bit, 2)
        bit *= 2
    return to


def from_at(a, s, count):
    if not isinstance(s, int) or count & (count - 1):
        return lax.rem(a - s + count, count)
    return to_at(a, s, count)


def kernel(
    nd, n,
    acts, grads, in_basis, out_basis, queries, lengths,
    out,
    acts_v, grads_v, ib_v, ob_v, q_v, len_v,
    row_send, row_recv, sketch_v, part_v, part_recv, sum_v, score_send, score_recv,
    acts_sem, grads_sem, basis_sem, row_ssem, row_rsem, part_ssem, part_rsem, score_ssem, score_rsem,
):
    z = lax.axis_index("dp")
    k = lax.axis_index("tensor")
    e_dev, length, _ = acts.shape
    rank = in_basis.shape[0]
    parts = n // e_dev
    rows = length // parts
    mine, c = k // parts, lax.rem(k, parts)
    feats = q_v.shape[1]
    nq = queries.shape[0]
    peers = nd * n
    me = z * n + k

    half = lax.rem(k, 2)

    def owner(s):
        pair, flip = s // 2, s % 2
        return lax.rem(k // 2 + pair, n // 2) * 2 + (lax.rem(half + 1, 2) if flip else half)

    def fetch(src, dst, sem, s):
        b = owner(s)
        return pltpu.make_async_copy(
            src.at[b // parts, pl.ds(pl.multiple_of(lax.rem(b, parts) * rows, rows), rows), :],
            dst.at[s], sem.at[s])

    order = [s for s in range(2, n)] + [1, 0]
    get_ib = pltpu.make_async_copy(in_basis, ib_v, basis_sem.at[0])
    get_ob = pltpu.make_async_copy(out_basis, ob_v, basis_sem.at[1])
    get_q = pltpu.make_async_copy(
        queries.at[:, pl.ds(pl.multiple_of(c * feats, feats), feats)], q_v, basis_sem.at[2])
    get_len = pltpu.make_async_copy(lengths, len_v, basis_sem.at[3])
    get_ib.start()
    for s in order:
        fetch(acts, acts_v, acts_sem, s).start()
    get_ob.start()
    for s in order[:DEPTH]:
        fetch(grads, grads_v, grads_sem, s).start()

    barrier = pltpu.get_barrier_semaphore()

    def greet(s):
        to = to_at(me, s, peers)
        pl.semaphore_signal(
            barrier, inc=1, device_id={"dp": to // n, "tensor": lax.rem(to, n)}, device_id_type=MESH)

    each(1, peers, greet)

    def row_copy(s):
        return pltpu.make_async_remote_copy(
            src_ref=row_send.at[s], dst_ref=row_recv.at[s],
            send_sem=row_ssem.at[s], recv_sem=row_rsem.at[s],
            device_id={"tensor": owner(s)}, device_id_type=MESH)

    get_ib.wait()
    for s in order:
        fetch(acts, acts_v, acts_sem, s).wait()
        row_send[s, :, :rank] = lax.dot_general(acts_v[s], ib_v[...], NT, preferred_element_type=jnp.float32)
    get_ob.wait()
    for i, s in enumerate(order):
        fetch(grads, grads_v, grads_sem, s).wait()
        if i + DEPTH < n:
            fetch(grads, grads_v, grads_sem, order[i + DEPTH]).start()
        elif i == n - 1:
            get_q.start()
            get_len.start()
        row_send[s, :, rank:] = lax.dot_general(grads_v[s], ob_v[...], NT, preferred_element_type=jnp.float32)
        if i == HELD:
            pl.semaphore_wait(barrier, peers - 1)
            for t in order[:i + 1]:
                if t:
                    row_copy(t).start()
        elif i > HELD and s:
            row_copy(s).start()

    get_len.wait()
    count = jnp.full((rows, 2 * rank), len_v[mine], jnp.int32)
    place = c * rows + lax.broadcasted_iota(jnp.int32, (rows, 2 * rank), 0)
    weight = jnp.where(place < count, lax.rsqrt(count.astype(jnp.float32)), 0.0)
    both = row_send[0]
    for s in order[:-1]:
        row_copy(s).wait_recv()
        both = both + row_recv[s]
    left, right = both[:, :rank] * weight[:, :rank], both[:, rank:]
    left = jnp.concatenate([left, left], axis=1)
    sketch_v[...] = lax.dot_general(
        right, left, (((0,), (0,)), ((), ())), precision=lax.Precision.HIGHEST, preferred_element_type=jnp.float32)

    lines = rank * rank // LANES
    per = LANES // rank
    lane = lax.broadcasted_iota(jnp.int32, (lines, LANES), 1)
    flat = sketch_v[pl.ds(0, lines, stride=per), :]
    for p in range(1, per):
        flat = jnp.where(lane < p * rank, flat, sketch_v[pl.ds(p, lines, stride=per), :])
    piece = lines // parts
    for p in range(parts):
        part_v[p] = flat[p * piece:(p + 1) * piece]

    group = nd * parts
    g = z * parts + c

    def part_copy(s, slot):
        to = to_at(g, s, group)
        return pltpu.make_async_remote_copy(
            src_ref=part_v.at[lax.rem(to, parts)], dst_ref=part_recv.at[slot],
            send_sem=part_ssem.at[s], recv_sem=part_rsem.at[s],
            device_id={"dp": to // parts, "tensor": mine * parts + lax.rem(to, parts)}, device_id_type=MESH)

    each(1, group, lambda s: part_copy(s, g).start())
    part_recv[g] = part_v[c]
    each(1, group, lambda s: part_copy(s, from_at(g, s, group)).wait_recv())

    def add_parts(d):
        total = part_recv[d * parts]
        for p in range(1, parts):
            total = total + part_recv[d * parts + p]
        sum_v[pl.ds(d * piece, piece), :] = total

    for d in range(nd):
        add_parts(d)
    sketch = jnp.concatenate(
        [sum_v[pl.ds(r, nd, stride=piece), :] for r in range(piece)], axis=1).astype(jnp.bfloat16)
    get_q.wait()
    scores = lax.dot_general(sketch, q_v[...], NT, preferred_element_type=jnp.float32)

    width = score_send.shape[-1]
    fit = width // nq
    if fit > 1:
        scores = jnp.concatenate([scores] * fit, axis=1)
        lane = lax.broadcasted_iota(jnp.int32, scores.shape, 1)
        first = lax.rem(z, fit) * nq
        scores = jnp.where((lane >= first) & (lane < first + nq), scores, 0.0)
    for d in range(nd):
        score_send[d] = scores[d:d + 1]

    def score_copy(s, slot):
        to = to_at(me, s, peers)
        return pltpu.make_async_remote_copy(
            src_ref=score_send.at[to // n], dst_ref=score_recv.at[slot],
            send_sem=score_ssem.at[s], recv_sem=score_rsem.at[s],
            device_id={"dp": to // n, "tensor": lax.rem(to, n)}, device_id_type=MESH)

    each(1, peers, lambda s: score_copy(s, me).start())
    score_recv[me] = score_send[z]
    each(1, peers, lambda s: score_copy(s, from_at(me, s, peers)).wait_recv())
    for line in range(nd // fit):
        for e in range(e_dev):
            total = None
            for d in range(line * fit, (line + 1) * fit):
                for p in range(parts):
                    term = score_recv[d * n + e * parts + p]
                    total = term if total is None else total + term
            out[e:e + 1, line * width:(line + 1) * width] = total

    for s in range(1, n):
        row_copy(s).wait_send()
    each(1, group, lambda s: part_copy(s, g).wait_send())
    each(1, peers, lambda s: score_copy(s, me).wait_send())


def local(nd, n, acts, grads, in_basis, out_basis, queries, lengths):
    e_dev, length, ka = acts.shape
    kg = grads.shape[2]
    rank = in_basis.shape[0]
    parts = n // e_dev
    rows = length // parts
    nq, feats = queries.shape
    lines = rank * rank // LANES
    width = max(LANES, nq)
    f32, bf16 = jnp.float32, jnp.bfloat16
    hbm = pl.BlockSpec(memory_space=pltpu.HBM)
    dma = pltpu.SemaphoreType.DMA
    return pl.pallas_call(
        functools.partial(kernel, nd, n),
        out_shape=jax.ShapeDtypeStruct((e_dev, nd * nq), f32),
        in_specs=[hbm] * 6,
        out_specs=pl.BlockSpec(memory_space=pltpu.VMEM),
        scratch_shapes=[
            pltpu.VMEM((n, rows, ka), bf16),
            pltpu.VMEM((n, rows, kg), bf16),
            pltpu.VMEM((rank, ka), bf16),
            pltpu.VMEM((rank, kg), bf16),
            pltpu.VMEM((nq, feats // parts), bf16),
            pltpu.SMEM((e_dev,), jnp.int32),
            pltpu.VMEM((n, rows, 2 * rank), f32),
            pltpu.VMEM((n, rows, 2 * rank), f32),
            pltpu.VMEM((rank, LANES), f32),
            pltpu.VMEM((parts, lines // parts, LANES), f32),
            pltpu.VMEM((nd * parts, lines // parts, LANES), f32),
            pltpu.VMEM((nd * lines // parts, LANES), f32),
            pltpu.VMEM((nd, 1, width), f32),
            pltpu.VMEM((nd * n, 1, width), f32),
            dma((n,)),
            dma((n,)),
            dma((4,)),
            dma((n,)),
            dma((n,)),
            dma((nd * parts,)),
            dma((nd * parts,)),
            dma((nd * n,)),
            dma((nd * n,)),
        ],
        compiler_params=pltpu.CompilerParams(
            collective_id=0, has_side_effects=True, vmem_limit_bytes=60 * 2**20),
        cost_estimate=pl.CostEstimate(
            flops=2 * e_dev * length * rank * (ka + kg),
            bytes_accessed=2 * (e_dev * length + rank) * (ka + kg) + 2 * nq * feats // parts,
            transcendentals=0),
    )(acts, grads, in_basis, out_basis, queries, lengths)


def solution(mesh):
    nd, n = mesh.shape["dp"], mesh.shape["tensor"]
    in_specs = (
        P(("groups", "dp"), None, "tensor"),
        P(("groups", "dp"), None, "tensor"),
        P(None, "tensor"),
        P(None, "tensor"),
        P("dp", None),
        P(("groups", "dp")),
    )
    out_specs = P(("groups", "dp"), None)
    return jax.shard_map(
        functools.partial(local, nd, n), mesh=mesh, in_specs=in_specs, out_specs=out_specs, check_vma=False)
```
